128 devices in a mesh: rep: 16 (over z_hi, y, core), shard: 8 (over x, z_lo).
Axes of the slice: x: 4, y: 4, z: 4 (z_hi: 2, z_lo: 2; z = z_hi * 2 + z_lo), core: 2. Of those that a mesh axis runs over, the one named last changes fastest.
Arguments:
- tokens: bfloat16 [16384, 2048], P(('rep', 'shard')), may hold values from -6 to 6
- segments: int32 [16384], replicated, may hold values from 0 to 79, as said below
- routes: int32 [16384, 1], P(('rep', 'shard')), may hold values from 0 to 1
- gate_scores: bfloat16 [16384, 1], P(('rep', 'shard')), may hold values from 0.59765625 to 1
- attn_gain: bfloat16 [2048], P('shard'), may hold values from 0.5 to 1.5
- w_query: bfloat16 [2048, 3072], P('shard'), may hold values from -0.125 to 0.125
- w_down_kv: bfloat16 [2048, 576], P('shard'), may hold values from -0.125 to 0.125
- kv_gain: bfloat16 [512], P('shard'), may hold values from 0.5 to 1.5
- w_up_kv: bfloat16 [512, 4096], P('shard'), may hold values from -0.25 to 0.25
- w_out: bfloat16 [2048, 2048], P('shard'), may hold values from -1.5 to 1.5
- ffn_gain: bfloat16 [2048], P('shard'), may hold values from 0.5 to 1.5
- w_gate: bfloat16 [4, 2048, 1408], P(None, None, 'shard'), may hold values from -0.125 to 0.125
- w_up: bfloat16 [4, 2048, 1408], P(None, None, 'shard'), may hold values from -0.125 to 0.125
- w_down: bfloat16 [4, 1408, 2048], P(None, 'shard'), may hold values from -0.21875 to 0.21875
- cotangent: bfloat16 [16384, 2048], P(('rep', 'shard')), may hold values from -6 to 6
Outputs:
- output: bfloat16 [16384, 2048], P(('rep', 'shard'))
- tokens_grad: float32 [16384, 2048], P(('rep', 'shard'))
- attn_gain_grad: float32 [2048], P('shard')
- w_query_grad: float32 [2048, 3072], P('shard')
- w_down_kv_grad: float32 [2048, 576], P('shard')
- kv_gain_grad: float32 [512], P('shard')
- w_up_kv_grad: float32 [512, 4096], P('shard')
- w_out_grad: float32 [2048, 2048], P('shard')
- ffn_gain_grad: float32 [2048], P('shard')
- w_gate_grad: float32 [4, 2048, 1408], P(None, None, 'shard')
- w_up_grad: float32 [4, 2048, 1408], P(None, None, 'shard')
- w_down_grad: float32 [4, 1408, 2048], P(None, 'shard')
The draws below stay inside these ranges and needn't reach their ends.
Inputs may be any that keep to these rules, and one draw needn't show every extreme that they name: `segments`: segment numbers never fall along the tokens, and no number is shared by two sequences of 1024 tokens.
All inputs are finite; a program needn't handle non-finite values.
Results may differ from the reference program's by a relative error of at most 0.025.
Values may be sent and summed in bfloat16 or wider, within the bound.
No kernel may reach another device: no remote copies, remote signals or barrier semaphores. Data moves between devices by JAX's collectives and lax.ppermute only.
A program may use at most 384 MiB of HBM per device.

```python
import math
import jax
import jax.numpy as jnp
from jax import lax

D = 2048
H = 16
DN = 128
DR = 64
DV = 128
KVL = 512
FF = 1408
SHARED = 2
EXPERTS = 2
TOPK = 1
SEQ = 1024
NE = 4
TOK_DEV = 128
TOKENS = 16384


def draw_segments(key, part):
    key = jax.random.fold_in(key, 7)
    first_key, second_key, third_key, fourth_key = jax.random.split(key, 4)
    groups = TOKENS // SEQ
    margin = max(TOK_DEV // 8, 1)
    begin_at = TOK_DEV - jax.random.randint(first_key, (groups, 1), 1, margin + 1)
    finish = SEQ - TOK_DEV + jax.random.randint(second_key, (groups, 1), 1, margin + 1)
    head_cut = jax.random.randint(third_key, (groups, 1), 1, begin_at + 1)
    tail_cut = jax.random.randint(fourth_key, (groups, 1), finish + 1, SEQ)
    places = jnp.arange(SEQ, dtype=jnp.int32)[None, :]
    inside = (places >= head_cut).astype(jnp.int32) + (places >= begin_at).astype(jnp.int32) + (places >= finish).astype(jnp.int32) + (places >= tail_cut).astype(jnp.int32)
    return (inside + 5 * jnp.arange(groups, dtype=jnp.int32)[:, None]).reshape(-1).astype(jnp.int32)


def level_of(key, shape, pieces, low, high):
    def one(dim, blocks):
        steps = jax.random.uniform(jax.random.fold_in(jax.random.fold_in(key, 6), dim), (blocks,), jnp.float32, low / len(pieces), high / len(pieces))
        return jnp.repeat(jnp.exp(steps), shape[dim] // blocks).reshape((-1,) + (1,) * (len(shape) - dim - 1))

    level = one(*pieces[0])
    for cut in pieces[1:]:
        level = level * one(*cut)
    return level


def distinct(stream_key, rows, count, top, lift):
    sequence = jax.random.permutation(jax.random.fold_in(stream_key, 1), count)
    pull = sequence
    for power in range(3):
        pull = pull * pull // count
    pull = pull * lift // count
    tickets = jax.random.randint(jax.random.fold_in(stream_key, 2), (rows, count), 0, 4096) + pull
    holders = jax.random.permutation(jax.random.fold_in(stream_key, 3), rows)[jnp.arange(count) % rows]
    tickets = jnp.where(jnp.arange(rows)[:, None] == holders[None, :], 1 << 14, tickets)
    score = tickets * count + jnp.arange(count)
    return lax.top_k(score.astype(jnp.int32), top)[1].astype(jnp.int32)


def normal_values(stream_key, shape, scale, reach, pieces=(), kind=jnp.bfloat16):
    values = scale * jax.random.normal(stream_key, shape, jnp.float32)
    if pieces:
        values = values * level_of(stream_key, shape, pieces, -0.22, 0.18)
    return jnp.clip(values, -reach, reach).astype(kind)


def setup_inputs(seed: int = 0) -> dict:
    keys = jax.random.split(jax.random.key(seed), 16)
    tokens = normal_values(keys[0], (TOKENS, D), 1.0, 6.0, ((0, 128),))
    segments = draw_segments(jax.random.fold_in(keys[15], 71), 0)
    routes = distinct(keys[2], TOKENS, EXPERTS, TOPK, 0)
    gate_scores = jnp.clip(jnp.exp(math.log(1.0) - 0.5147395 * jax.random.uniform(keys[3], (TOKENS, TOPK), jnp.float32) ** level_of(keys[3], (TOKENS, TOPK), ((0, 128),), -0.2, 0.2)), 0.59765625, 1.0).astype(jnp.bfloat16)
    attn_gain = jnp.clip(1.0 + 0.1 * jax.random.normal(keys[4], (D,), jnp.float32), 0.5, 1.5).astype(jnp.bfloat16)
    w_query = normal_values(keys[5], (D, H * (DN + DR)), D ** -0.5, 0.125, ((0, 8),))
    w_down_kv = normal_values(keys[6], (D, KVL + DR), D ** -0.5, 0.125, ((0, 8),))
    kv_gain = jnp.clip(1.0 + 0.1 * jax.random.normal(keys[7], (KVL,), jnp.float32), 0.5, 1.5).astype(jnp.bfloat16)
    w_up_kv = normal_values(keys[8], (KVL, H * (DN + DV)), KVL ** -0.5, 0.25, ((0, 8),))
    w_out = normal_values(keys[9], (H * DV, D), (max(H * DV // 128, 1)) ** -0.5, 1.5, ((0, 8),))
    ffn_gain = jnp.clip(1.0 + 0.1 * jax.random.normal(keys[10], (D,), jnp.float32), 0.5, 1.5).astype(jnp.bfloat16)
    w_gate = normal_values(keys[11], (NE, D, FF), D ** -0.5, 0.125, ((2, 8),))
    w_up = normal_values(keys[12], (NE, D, FF), D ** -0.5, 0.125, ((2, 8),))
    w_down = normal_values(keys[13], (NE, FF, D), (FF // 2) ** -0.5, 0.21875, ((1, 8),))
    cotangent = normal_values(keys[14], (TOKENS, D), 1.0, 6.0, ((0, 128),))
    return dict(tokens=tokens, segments=segments, routes=routes, gate_scores=gate_scores, attn_gain=attn_gain, w_query=w_query, w_down_kv=w_down_kv, kv_gain=kv_gain, w_up_kv=w_up_kv, w_out=w_out, ffn_gain=ffn_gain, w_gate=w_gate, w_up=w_up, w_down=w_down, cotangent=cotangent)


norm_eps = 1e-06
rope_base = 10000.0
masked_score = -1e+30
highest = lax.Precision.HIGHEST

@jax.custom_vjp
def low(v):
    return lax.optimization_barrier(v.astype(jnp.bfloat16)).astype(jnp.float32)

@jax.custom_vjp
def low_back(v):
    return v

def low_keep(v):
    return (low(v), None)

def low_pass(kept, grad):
    return (grad,)

def back_keep(v):
    return (v, None)

def back_low(kept, grad):
    return (low(grad),)
low.defvjp(low_keep, low_pass)
low_back.defvjp(back_keep, back_low)

def rms_norm(values):
    return values * lax.rsqrt(lax.optimization_barrier(jnp.mean(values * values, axis=-1, keepdims=True)) + norm_eps)

def rotary_tables(places, width):
    half_width = width // 2
    inverse = jnp.exp(-jnp.log(rope_base) * (2.0 * jnp.arange(half_width, dtype=jnp.float32) / width))
    turns = places.astype(jnp.float32)[:, None] * inverse[None, :]
    cosine = jnp.cos(turns)
    sine_tab = jnp.sin(turns)
    return (jnp.concatenate([cosine, cosine], -1), jnp.concatenate([sine_tab, sine_tab], -1))

def rotate(values, cosine, sine_tab):
    half_width = values.shape[-1] // 2
    turned = jnp.concatenate([-values[..., half_width:], values[..., :half_width]], -1)
    return values * cosine + turned * sine_tab

def layer_forward(hidden_in, params, seg_ids, combine, cosine, sine_tab):
    attn_gain, w_query, w_down_kv, kv_gain, w_up_kv, w_out, ffn_gain, w_gate, w_up, w_down = params
    length = hidden_in.shape[0]
    normed = low(rms_norm(hidden_in) * attn_gain)
    query_pre = low_back(jnp.dot(normed, w_query, precision=highest)).reshape(length, H, DN + DR)
    queries = low(jnp.concatenate([query_pre[..., :DN], rotate(query_pre[..., DN:], cosine[:, None, :], sine_tab[:, None, :])], -1))
    latent_all = low_back(jnp.dot(normed, w_down_kv, precision=highest))
    latent = low(rms_norm(latent_all[:, :KVL]) * kv_gain)
    key_rope = low(rotate(latent_all[:, KVL:], cosine, sine_tab))
    key_value = low(low_back(jnp.dot(latent, w_up_kv, precision=highest))).reshape(length, H, DN + DV)
    key_full = jnp.concatenate([key_value[..., :DN], jnp.broadcast_to(key_rope[:, None, :], (length, H, DR))], -1)
    values = key_value[..., DN:]
    scores = low_back(jnp.einsum('ihd,jhd->hij', queries, key_full, precision=highest) * (DN + DR) ** (-0.5))
    places = jnp.arange(length)
    allowed = (places[None, :] <= places[:, None]) & (seg_ids[None, :] == seg_ids[:, None])
    attention = low(jax.nn.softmax(jnp.where(allowed[None], scores, masked_score), axis=-1))
    context = jnp.einsum('hij,jhd->ihd', attention, values, precision=highest).reshape(length, H * DV)
    context = low(low_back(context))
    residual = hidden_in + low_back(jnp.dot(context, w_out, precision=highest))
    ffn_in = low(rms_norm(residual) * ffn_gain)
    gate_pre = low_back(jnp.einsum('td,edf->etf', ffn_in, w_gate, precision=highest))
    up_pre = low_back(jnp.einsum('td,edf->etf', ffn_in, w_up, precision=highest))
    hidden_units = low(gate_pre * jax.nn.sigmoid(gate_pre) * up_pre * combine.T[:, :, None])
    return residual + jnp.einsum('etf,efd->td', hidden_units, w_down, precision=highest)

def reference(tokens, segments, routes, gate_scores, attn_gain, w_query, w_down_kv, kv_gain, w_up_kv, w_out, ffn_gain, w_gate, w_up, w_down, cotangent):
    params = tuple((weight.astype(jnp.float32) for weight in (attn_gain, w_query, w_down_kv, kv_gain, w_up_kv, w_out, ffn_gain, w_gate, w_up, w_down)))
    cosine, sine_tab = rotary_tables(jnp.arange(SEQ, dtype=jnp.int32), DR)
    chosen = routes[:, :, None] == jnp.arange(EXPERTS, dtype=jnp.int32)[None, None, :]
    routed = lax.optimization_barrier(jnp.sum(jnp.where(chosen, gate_scores.astype(jnp.float32)[:, :, None], jnp.float32(0.0)), axis=1))
    combine = jnp.concatenate([jnp.ones((TOKENS, SHARED), jnp.float32), routed], axis=1)
    seq_count = TOKENS // SEQ
    items = (tokens.astype(jnp.float32).reshape(seq_count, SEQ, D), cotangent.astype(jnp.float32).reshape(seq_count, SEQ, D), segments.reshape(seq_count, SEQ), combine.reshape(seq_count, SEQ, SHARED + EXPERTS))

    def one_sequence(totals, item):
        hidden_in, grad_out, seg_ids, comb_rows = item

        def forward(hidden_x, *weights):
            return layer_forward(hidden_x, weights, seg_ids, comb_rows, cosine, sine_tab)
        result, pullback = jax.vjp(forward, hidden_in, *params)
        grads = pullback(grad_out)
        totals = tuple((total + grad for total, grad in zip(totals, grads[1:])))
        return (totals, (result.astype(jnp.bfloat16), grads[0]))
    start_totals = tuple((jnp.zeros_like(weight) for weight in params))
    totals, (results, input_grads) = lax.scan(one_sequence, start_totals, items)
    return (results.reshape(TOKENS, D), input_grads.reshape(TOKENS, D), totals[0], totals[1], totals[2], totals[3], totals[4], totals[5], totals[6], totals[7], totals[8], totals[9])
```

```python
import functools

import jax
import jax.numpy as jnp
from jax import lax
from jax.experimental import pallas as pl
from jax.experimental.pallas import tpu as pltpu
from jax.sharding import Mesh
from jax.sharding import PartitionSpec as P

H = 16
DN = 128
DR = 64
DV = 128
KVL = 512
SHARED = 2
EXPERTS = 2

REP = ("zh", "y", "core")
SHARD = ("x", "zl")

norm_eps = 1e-06
rope_base = 10000.0
masked_score = -1e30
f32 = jnp.float32
bf16 = jnp.bfloat16


def norm_parts(values):
    inverse = lax.rsqrt(jnp.mean(values * values, axis=-1, keepdims=True) + norm_eps)
    return (values * inverse, inverse)


def norm_back(grad_normed, normed, inverse):
    return inverse * (grad_normed - normed * jnp.mean(grad_normed * normed, axis=-1, keepdims=True))


def rotary_tables(places, width):
    half_width = width // 2
    inverse = jnp.exp(-jnp.log(rope_base) * (2.0 * jnp.arange(half_width, dtype=f32) / width))
    turns = places.astype(f32)[:, None] * inverse[None, :]
    cosine = jnp.cos(turns)
    sine_tab = jnp.sin(turns)
    return (jnp.concatenate([cosine, cosine], -1), jnp.concatenate([sine_tab, sine_tab], -1))


def dot(a, b, dims):
    return lax.dot_general(a, b, ((dims[:1], dims[1:]), ((), ())), preferred_element_type=f32)


def right(v):
    size = lax.axis_size("x")
    return lax.ppermute(v, "x", [(i, (i + 1) % size) for i in range(size)])


def left(v):
    size = lax.axis_size("x")
    return lax.ppermute(v, "x", [(i, (i - 1) % size) for i in range(size)])


def flip(v):
    return lax.ppermute(v, "zl", [(0, 1), (1, 0)])


def to_relative(v):
    v = v.reshape((4, 2) + v.shape[1:])
    v = lax.dynamic_slice_in_dim(jnp.concatenate([v, v], 0), lax.axis_index("x"), 4, 0)
    v = jnp.where(lax.axis_index("zl") == 0, v, v[:, ::-1])
    v = jnp.swapaxes(v.reshape((4, 2, 2, v.shape[2] // 2) + v.shape[3:]), 1, 2)
    return v.reshape((-1,) + v.shape[4:])


def whole_first(v):
    return {(0, 0): v, (3, 0): right(v), (0, 1): flip(v), (1, 0): left(v)}


def whole_second(got):
    more = {(2, 0): right(got[3, 0]), (3, 1): flip(got[3, 0]), (1, 1): left(got[0, 1])}
    return {**got, **more}


def whole_third(got):
    return {**got, (2, 1): left(got[1, 1])}


def gather_pairs(v, tie=None, first=(), last=None):
    other, before, after, _ = lax.optimization_barrier((flip(v), right(v), left(v), first))
    got = {(0, 0): v, (0, 1): other, (3, 0): before, (1, 0): after}
    got[2, 0] = right(before)
    got[3, 1], got[1, 1] = right(other), left(other)
    if tie is not None:
        got[2, 0], tie = lax.optimization_barrier((got[2, 0], tie))
    got[2, 1] = left(got[1, 1])
    if last is not None:
        got[2, 1], tie = lax.optimization_barrier((got[2, 1], last(tie)))
    got = [(got[x, z], ((x, 0, z), (x, 1, z))) for z in range(2) for x in range(4)]
    return got if tie is None else (got, tie)


def scatter_parts(v):
    unit = v.shape[0] // 8
    return {(x, h): v[(2 * x + h) * unit : (2 * x + h + 1) * unit] for x in range(4) for h in range(2)}


def scatter_sends(part):
    return (left(part[2, 0]), right(part[2, 1]), right(part[1, 0]), left(part[3, 1]))


def scatter_first(v):
    part = scatter_parts(v)
    return part, scatter_sends(part)


def scatter_second(part, sent):
    far_a, far_b, near_a, near_b = sent
    low = add(part[3, 0], far_a).astype(bf16)
    high = add(part[1, 1], far_b).astype(bf16)
    low, high = lax.optimization_barrier((low, high))
    return (part[0, 0], part[0, 1], near_a, near_b), (left(low), right(high))


def scatter_third(own, sent):
    half = own[0].shape[0] // 2
    a = add(own[0], own[2], sent[0])
    b = add(own[1], own[3], sent[1])
    other = flip(jnp.concatenate([a[half:], b[half:]], 0).astype(bf16))
    return jnp.concatenate([a[:half], b[:half]], 0), other


def merged_rows(v, works=((), (), ())):
    tie = lax.optimization_barrier
    done = []

    def beside(n, sent):
        if works[n]:
            sent, got = tie((sent, works[n](done)))
            done.append(got)
        return sent

    part, sent = scatter_first(v)
    half = part[0, 0].shape[0] // 2
    far, near = sent[:2], sent[2:]
    far = beside(0, far)
    low, high = add(part[3, 0], far[0]), add(part[1, 1], far[1])
    side = flip(jnp.concatenate([low[half:], high[half:]], 0).astype(bf16))
    low, high = low[:half].astype(bf16), high[:half].astype(bf16)
    side, near = beside(1, tie((side, near)))
    low = add(low, side[:half]).astype(bf16)
    high = add(high, side[half:]).astype(bf16)
    own_a, own_b = add(part[0, 0], near[0]), add(part[0, 1], near[1])
    across = jnp.concatenate([own_a[half:], own_b[half:]], 0).astype(bf16)
    low, high, across = tie((low, high, across))
    last = beside(2, (flip(across), left(low), right(high)))
    own = jnp.concatenate([own_a[:half], own_b[:half]], 0)
    out = add(own, last[0], jnp.concatenate(last[1:], 0))
    return (out, *done) if done else out


def add(*terms):
    return sum(t.astype(f32) for t in terms)


def swap(v):
    return lax.ppermute(v, "core", [(0, 1), (1, 0)])


def hop(v):
    return lax.ppermute(v, "zh", [(0, 1), (1, 0)])


def up(v):
    size = lax.axis_size("y")
    return lax.ppermute(v, "y", [(i, (i + 1) % size) for i in range(size)])


def down(v):
    size = lax.axis_size("y")
    return lax.ppermute(v, "y", [(i, (i - 1) % size) for i in range(size)])


def pick(v, index, axis):
    return lax.dynamic_index_in_dim(v, index, axis, keepdims=False)


def ring_gather(v):
    if lax.axis_size("y") == 1:
        return [(0, 0, v)]
    half = v.shape[0] // 2
    before, after = up(v), down(v)
    across = up(before[:half]), down(after[half:])
    return [(0, 0, v), (1, 0, after), (3, 0, before), (2, 0, across[0]), (2, half, across[1])]


def ring_first(p):
    if len(p) == 1:
        return ()
    half = p[0].shape[0] // 2
    return (down(p[2][:half]), up(p[2][half:]))


def ring_second(p, sent):
    if len(p) == 1:
        return (p[0],)
    half = p[0].shape[0] // 2
    low = jnp.concatenate([add(p[3][:half], sent[0]).astype(bf16), p[3][half:]], 0)
    high = jnp.concatenate([p[1][:half], add(p[1][half:], sent[1]).astype(bf16)], 0)
    return (p[0], down(low), up(high))


def rep_gather(v):
    zh = lax.axis_index("zh")
    highs, cores = lax.axis_size("zh"), lax.axis_size("core")
    pair = v
    if highs > 1:
        other = hop(v)
        pair = jnp.where(zh == 0, jnp.concatenate([v, other], 0), jnp.concatenate([other, v], 0))
    pieces = []
    for block in ring_gather(pair):
        pieces += [block, swap(block)] if cores > 1 else [block]
    return pieces


def scatter_rows(v, tie=None):
    part, sent = scatter_first(v)
    if tie is not None:
        sent, tie = lax.optimization_barrier((sent, tie))
    out = add(*scatter_third(*scatter_second(part, sent)))
    return out if tie is None else (out, tie)


MIB = 1 << 20
VM = pl.BlockSpec(memory_space=pltpu.VMEM)
SM = pl.BlockSpec(memory_space=pltpu.SMEM)


def on_core(kernel, outs, in_specs, flops, byts, scratch=(), **more):
    return pl.pallas_call(
        kernel,
        out_shape=outs,
        in_specs=in_specs,
        out_specs=jax.tree.map(lambda _: VM, outs),
        scratch_shapes=list(scratch),
        compiler_params=pltpu.CompilerParams(vmem_limit_bytes=56 * MIB),
        cost_estimate=pl.CostEstimate(flops=flops, bytes_accessed=byts, transcendentals=0),
        **more,
    )


def chunk_kernel(at_ref, query_ref, down_ref, up_ref, row_ref, out_ref, *, sub, qw, kvw):
    begin = pl.multiple_of(at_ref[4], sub)
    piece = min(sub, up_ref.shape[0])
    query = query_ref[pl.ds(begin, sub), :]
    down = down_ref[pl.ds(begin, sub), :]
    parts = out_ref.shape[0]
    lanes = 128
    cols = up_ref.shape[1] // parts
    shared = jnp.concatenate([down, down[:, kvw - DR :]], 1)
    row = jnp.broadcast_to(row_ref[...], (out_ref.shape[1] - sub, out_ref.shape[2]))
    for d in range(parts):
        out_ref[d, :sub, :qw] = query[:, d * qw : (d + 1) * qw]
        out_ref[d, :sub, qw : qw + kvw + DR] = shared
        out_ref[d, sub:, :] = row
    for k in range(sub // piece):
        spot = begin + k * piece
        group = spot // up_ref.shape[0]
        first = pl.multiple_of(lax.rem(spot, up_ref.shape[0]), piece)
        for d in range(parts):
            col = pl.multiple_of(d * cols + group * lanes, lanes)
            out_ref[d, k * piece : (k + 1) * piece, qw + kvw + DR :] = up_ref[
                pl.ds(first, piece), pl.ds(col, lanes)
            ]


def weights_kernel(at_ref, *refs, places, cores, sub, spots):
    blocks, (cat_ref, up_ref) = refs[: len(spots)], refs[len(spots) :]
    y, core = at_ref[2], at_ref[3]
    parts = max(low + ref.shape[0] for ref, (_, low, _) in zip(blocks, spots))
    d_rows = cat_ref.shape[0] // parts
    kv_rows = up_ref.shape[0] // parts
    cat = cat_ref.shape[1]
    piece = min(sub, kv_rows)
    for ref, (step, low_d, n) in zip(blocks, spots):
        spot = lax.rem(y + step, places) * cores
        first = (spot + (core if n == 0 else 1 - core)) * sub
        for k_d in range(ref.shape[0]):
            d = low_d + k_d
            cat_ref[pl.ds(pl.multiple_of(d * d_rows + first, sub), sub), :] = ref[k_d, :sub, :cat]
            for k in range(sub // piece):
                row = first + k * piece
                low = pl.multiple_of(d * kv_rows + lax.rem(row, kv_rows), piece)
                col = pl.multiple_of(row // kv_rows * 128, 128)
                up_ref[pl.ds(low, piece), pl.ds(col, 128)] = ref[
                    k_d, k * piece : (k + 1) * piece, cat:
                ]


def norm_kernel(gain_ref, *refs, spots):
    blocks, out_ref = refs[:-1], refs[-1]
    half = out_ref.shape[0] // 16
    step = 16
    gain = gain_ref[...]
    for ref, where in zip(blocks, spots):
        for n, spot in enumerate(where):

            def body(i, carry):
                row = pl.multiple_of(i * step, step)
                values = ref[pl.ds(n * half + row, step), :].astype(f32)
                inverse = lax.rsqrt(jnp.mean(values * values, axis=-1, keepdims=True) + norm_eps)
                out_ref[pl.ds(spot * half + row, step), :] = (values * inverse * gain).astype(bf16)
                return carry

            lax.fori_loop(0, half // step, body, 0, unroll=4)


def assemble_kernel(*refs, spots):
    blocks, out_ref = refs[:-1], refs[-1]
    half = out_ref.shape[0] // 16
    for ref, where in zip(blocks, spots):
        for n, spot in enumerate(where):
            out_ref[spot * half : (spot + 1) * half, :] = ref[n * half : (n + 1) * half, :]


def spots_of(blocks):
    return [[(2 * x + h) * 2 + z for x, h, z in where] for _, where in blocks]


def assemble(blocks):
    width = blocks[0][0].shape[1]
    rows = 8 * blocks[0][0].shape[0]
    kernel = functools.partial(assemble_kernel, spots=spots_of(blocks))
    out = jax.ShapeDtypeStruct((rows, width), bf16)
    return on_core(kernel, out, [VM] * len(blocks), 0, 4 * rows * width)(*[v for v, _ in blocks])


def spots(at_ref, low):
    size = SPAN // 4
    base = lax.rem(low // SPAN - at_ref[0] + 4, 4) * SPAN
    for z in range(2):
        other = at_ref[1] if z == 0 else 1 - at_ref[1]
        for h in range(2):
            yield pl.ds(pl.multiple_of(base + h * 2 * size + other * size, size), size)


def read_rows(at_ref, ref, low, cols):
    return jnp.concatenate([ref[spot, cols] for spot in spots(at_ref, low)], 0)


def write_rows(at_ref, ref, low, cols, value):
    size = SPAN // 4
    for n, spot in enumerate(spots(at_ref, low)):
        ref[spot, cols] = value[n * size : (n + 1) * size]


def turn_lanes(v):
    lane = lax.broadcasted_iota(jnp.int32, v.shape, 1) % DR
    return jnp.where(lane < DR // 2, -pltpu.roll(v, 128 - DR // 2, 1), pltpu.roll(v, DR // 2, 1))


def head_mask(shape, h):
    lane = lax.broadcasted_iota(jnp.int32, shape, 1)
    return lane >= DR if h == 0 else lane < DR


SPAN = 256
SCALE = (DN + DR) ** (-0.5)


def head_query(q_ref, h, low):
    rope = q_ref[low : low + SPAN, 2 * DN : 2 * DN + 128]
    rope = jnp.where(head_mask(rope.shape, h), rope, jnp.zeros_like(rope))
    return jnp.concatenate([q_ref[low : low + SPAN, h * DN : (h + 1) * DN], rope], 1)


def head_keys(kv_ref, kr_ref, h, count):
    return jnp.concatenate([kv_ref[:count, h * 256 : h * 256 + DN], kr_ref[:count, :]], 1)


def allowed_block(idc_ref, idr_ref, low, count):
    row = lax.broadcasted_iota(jnp.int32, (SPAN, count), 0) + low
    col = lax.broadcasted_iota(jnp.int32, (SPAN, count), 1)
    return (col <= row) & (idc_ref[low : low + SPAN, :] == idr_ref[:, :count])


def forward_kernel(
    at_ref, pre_ref, gain_ref, up_ref, cos_ref, sin_ref, idc_ref, idr_ref,
    q_ref, lat_ref, kv_ref, kr_ref, lse_ref, ctx_ref,
):
    length = pre_ref.shape[0]
    for low in range(0, length, SPAN):
        rows = slice(low, low + SPAN)
        cosine, sine = cos_ref[rows, :], sin_ref[rows, :]
        pre = read_rows(at_ref, pre_ref, low, slice(None))
        mid = pltpu.roll(pre[:, DN : DN + 256], 256 - DR, 1)
        rope = mid[:, 128:]
        q_ref[rows, :DN] = pre[:, :DN].astype(bf16)
        q_ref[rows, DN : 2 * DN] = mid[:, :DN].astype(bf16)
        q_ref[rows, 2 * DN :] = (rope * cosine + turn_lanes(rope) * sine).astype(bf16)
        lat = pre[:, 384 : 384 + KVL]
        inverse = lax.rsqrt(jnp.mean(lat * lat, axis=-1, keepdims=True) + norm_eps)
        latent = (lat * inverse * gain_ref[...]).astype(bf16)
        lat_ref[rows, :] = latent
        rope = pre[:, 384 + KVL :]
        kr_ref[rows, :] = (rope * cosine + turn_lanes(rope) * sine).astype(bf16)
        kv_ref[rows, :] = dot(latent, up_ref[...], (1, 0)).astype(bf16)
    for low in range(0, length, SPAN):
        count = low + SPAN
        allowed = allowed_block(idc_ref, idr_ref, low, count)
        for h in range(2):
            scores = dot(head_query(q_ref, h, low), head_keys(kv_ref, kr_ref, h, count), (1, 1))
            scores = jnp.where(allowed, scores * SCALE, masked_score)
            top = jnp.max(scores, axis=-1, keepdims=True)
            expo = jnp.exp(scores - top)
            total = jnp.sum(expo, axis=-1, keepdims=True)
            lse_ref[h, low:count, :] = jnp.broadcast_to(top + jnp.log(total), (SPAN, 128))
            probs = (expo * (1.0 / total)).astype(bf16)
            values = kv_ref[:count, h * 256 + DN : (h + 1) * 256]
            context = dot(probs, values, (1, 0)).astype(bf16)
            write_rows(at_ref, ctx_ref, low, slice(h * DV, (h + 1) * DV), context)


def backward_kernel(
    at_ref, gctx_ref, q_ref, kv_ref, kr_ref, lse_ref, pre_ref, gain_ref, up_ref, cos_ref, sin_ref,
    idc_ref, idr_ref, gp_ref, gkv_ref, dq_ref, dqr_ref, dk_ref, dv_ref, dkr_ref,
):
    length = gctx_ref.shape[0]
    for h in range(2):
        for low in reversed(range(0, length, SPAN)):
            count = low + SPAN
            allowed = allowed_block(idc_ref, idr_ref, low, count)
            query = head_query(q_ref, h, low)
            keys = head_keys(kv_ref, kr_ref, h, count)
            scores = jnp.where(allowed, dot(query, keys, (1, 1)) * SCALE, masked_score)
            probs = jnp.exp(scores - lse_ref[h, low:count, :1])
            grad_ctx = read_rows(at_ref, gctx_ref, low, slice(h * DV, (h + 1) * DV))
            values = kv_ref[:count, h * 256 + DN : (h + 1) * 256]
            grad_probs = dot(grad_ctx, values, (1, 1))
            row_dot = jnp.sum(probs * grad_probs, axis=-1, keepdims=True)
            grad_scores = (probs * (grad_probs - row_dot)).astype(bf16)
            grad_query = dot(grad_scores, keys, (1, 0))
            dq_ref[low:count, h * DN : (h + 1) * DN] = grad_query[:, :DN]
            rope = jnp.where(head_mask((SPAN, 128), h), grad_query[:, DN:], 0.0)
            dqr_ref[low:count, :] = rope if h == 0 else dqr_ref[low:count, :] + rope
            grad_keys = dot(grad_scores, query, (0, 0))
            grad_values = dot(probs.astype(bf16), grad_ctx, (0, 0))
            if count == length:
                dk_ref[...] = grad_keys
                dv_ref[...] = grad_values
            else:
                dk_ref[:count, :] = dk_ref[:count, :] + grad_keys
                dv_ref[:count, :] = dv_ref[:count, :] + grad_values
        gkv_ref[:, h * 256 : h * 256 + DN] = (dk_ref[:, :DN] * SCALE).astype(bf16)
        gkv_ref[:, h * 256 + DN : (h + 1) * 256] = dv_ref[...].astype(bf16)
        rope = dk_ref[:, DN:]
        dkr_ref[...] = rope if h == 0 else dkr_ref[...] + rope
    for low in range(0, length, SPAN):
        rows = slice(low, low + SPAN)
        cosine, sine = cos_ref[rows, :], sin_ref[rows, :]
        grad_query = (dq_ref[rows, :DN] * SCALE).astype(bf16)
        write_rows(at_ref, gp_ref, low, slice(0, DN), grad_query)
        rope = dqr_ref[rows, :] * SCALE
        rope = rope * cosine - turn_lanes(rope) * sine
        mid = jnp.concatenate([dq_ref[rows, DN : 2 * DN] * SCALE, rope], 1)
        mid = pltpu.roll(mid, DR, 1).astype(bf16)
        write_rows(at_ref, gp_ref, low, slice(DN, DN + 256), mid)
        grad_latent = dot(gkv_ref[rows, :], up_ref[...], (1, 1)) * gain_ref[...]
        lat = read_rows(at_ref, pre_ref, low, slice(384, 384 + KVL))
        inverse = lax.rsqrt(jnp.mean(lat * lat, axis=-1, keepdims=True) + norm_eps)
        normed = lat * inverse
        inner = jnp.mean(grad_latent * normed, axis=-1, keepdims=True)
        grad_latent = (inverse * (grad_latent - normed * inner)).astype(bf16)
        write_rows(at_ref, gp_ref, low, slice(384, 384 + KVL), grad_latent)
        rope = dkr_ref[rows, :]
        rope = (rope + pltpu.roll(rope, DR, 1)) * SCALE
        rope = rope * cosine - turn_lanes(rope) * sine
        rope = jnp.where(head_mask(rope.shape, 1), rope, 0.0).astype(bf16)
        write_rows(at_ref, gp_ref, low, slice(384 + KVL, 512 + KVL), rope)


def sends_kernel(
    at_ref, normed_ref, gp_ref, cat_ref, upp_ref, up_ref, one_ref, kv_ref, two_ref, part_ref,
    *refs, places, cores, parts,
):
    outs, all_ref = refs[:-1], refs[-1]
    d = pl.program_id(0)
    d_rows = all_ref.shape[0]

    @pl.when(d < parts)
    def _():
        part = dot(normed_ref[...], gp_ref[...], (0, 0))
        wide = part.shape[1]
        one = jnp.sum(part * cat_ref[...].astype(f32), axis=-1, keepdims=True) / one_ref[...]
        kv = jnp.sum(upp_ref[...] * up_ref[...].astype(f32), axis=-1, keepdims=True) / kv_ref[...]
        all_ref[:, : wide - 128] = part[:, : wide - 128].astype(bf16)
        count = kv.shape[0]
        lane = lax.broadcasted_iota(jnp.int32, (count, 128), 1)
        for g in range(d_rows // count):
            rows = slice(g * count, (g + 1) * count)
            last = jnp.where(lane < 64, part[rows, wide - 128 :], 0.0)
            last = jnp.where(lane == 64, one[rows, :], last)
            last = jnp.where(lane == 65, two_ref[rows, :], last)
            if g == 0:
                last = jnp.where(lane == 66, kv, last)
            all_ref[rows, wide - 128 : wide] = last.astype(bf16)
            all_ref[rows, wide:] = upp_ref[:, g * 128 : (g + 1) * 128].astype(bf16)

    @pl.when(d >= parts)
    def _():
        all_ref[:, : part_ref.shape[1]] = part_ref[...]

    size = d_rows // (places * cores)
    y, core = at_ref[2], at_ref[3]
    for r in range(places):
        spot = lax.rem(y + r, places) * cores
        for n, ref in enumerate(outs):
            first = (spot + (core if n == 0 else 1 - core)) * size
            ref[r, 0] = all_ref[pl.ds(pl.multiple_of(first, size), size), :]


def expert_pack_kernel(at_ref, *refs, cores):
    parts, outs = refs[:3], refs[3:]
    size = parts[0].shape[0] // cores
    core = at_ref[3]
    for n, out_ref in enumerate(outs):
        first = (core if n == 0 else 1 - core) * size
        rows = pl.ds(pl.multiple_of(first, 16), size)
        for k, ref in enumerate(parts):
            out_ref[0, k * size : (k + 1) * size, :] = ref[rows, :]


def expert_unpack_kernel(at_ref, *refs, cores):
    blocks, outs = refs[:cores], refs[-3:]
    size = blocks[0].shape[0] // 3
    core = at_ref[3]
    for n, ref in enumerate(blocks):
        first = (core if n == 0 else 1 - core) * size
        rows = pl.ds(pl.multiple_of(first, 16), size)
        for k, out_ref in enumerate(outs):
            out_ref[rows, :] = ref[k * size : (k + 1) * size, :].astype(f32)


def expert_pack(at, parts, places, cores):
    rows, width = parts[0].shape
    cols = width // places
    out = jax.ShapeDtypeStruct((places, 3 * rows // cores, cols), bf16)
    return pl.pallas_call(
        functools.partial(expert_pack_kernel, cores=cores),
        out_shape=[out] * cores,
        grid_spec=pltpu.PrefetchScalarGridSpec(
            num_scalar_prefetch=1,
            grid=(places,),
            in_specs=[pl.BlockSpec((rows, cols), lambda r, at: (0, lax.rem(at[2] + r, places)))] * 3,
            out_specs=[pl.BlockSpec((1,) + out.shape[1:], lambda r, at: (r, 0, 0))] * cores,
        ),
        compiler_params=pltpu.CompilerParams(vmem_limit_bytes=40 * MIB),
        cost_estimate=pl.CostEstimate(flops=0, bytes_accessed=16 * MIB, transcendentals=0),
    )(at, *parts)


def expert_unpack(at, step, blocks, held, places, rows, width):
    cores = len(blocks)
    cols = width // places
    out = jax.ShapeDtypeStruct((rows, width), f32)
    held = list(held)
    return pl.pallas_call(
        functools.partial(expert_unpack_kernel, cores=cores),
        out_shape=[out] * 3,
        grid_spec=pltpu.PrefetchScalarGridSpec(
            num_scalar_prefetch=1,
            grid=(1,),
            in_specs=[pl.BlockSpec(blocks[0].shape, lambda i, at: (0, 0))] * cores
            + [pl.BlockSpec(memory_space=pl.ANY)] * len(held),
            out_specs=[pl.BlockSpec((rows, cols), lambda i, at: (0, lax.rem(at[2] + step, places)))] * 3,
        ),
        input_output_aliases={1 + cores + k: k for k in range(len(held))},
        compiler_params=pltpu.CompilerParams(vmem_limit_bytes=40 * MIB),
        cost_estimate=pl.CostEstimate(flops=0, bytes_accessed=6 * MIB, transcendentals=0),
    )(at, *blocks, *held)


def join_kernel(own_ref, part_ref, out_ref, *, qw, cat):
    parts = own_ref.shape[0]
    mid = parts * qw
    end = mid + cat - qw
    total = jnp.zeros((own_ref.shape[1], cat - qw), f32)
    for d in range(parts):
        out_ref[:, d * qw : (d + 1) * qw] = own_ref[d, :, :qw]
        total = total + own_ref[d, :, qw:cat].astype(f32)
        out_ref[:, end + d * 128 : end + (d + 1) * 128] = own_ref[d, :, cat:]
    out_ref[:, mid:end] = total.astype(bf16)
    first = end + parts * 128
    for n in range(part_ref.shape[0]):
        out_ref[:, first + n * cat : first + (n + 1) * cat] = part_ref[n, :, :cat]


def unpack_kernel(at_ref, *refs, places, cores, size, parts):
    blocks, outs = refs[: places * cores], refs[places * cores :]
    query_ref, down_ref, one_ref, two_ref, kv_ref, up_ref, out_ref, mid_ref = outs
    qw, kvw = query_ref.shape[1], down_ref.shape[0]
    kv_rows = up_ref.shape[0]
    kv_cols = up_ref.shape[1] // parts
    mid = qw + kvw + 64
    piece = min(size, kv_rows)
    y, core = at_ref[2], at_ref[3]
    for n, ref in enumerate(blocks):
        spot = lax.rem(y + n // cores, places) * cores
        spot = spot + (core if n % cores == 0 else 1 - core)
        first = pl.multiple_of(spot * size, size)
        rows = pl.ds(first, size)
        query_ref[rows, :] = ref[:, :qw].astype(f32)
        mid_ref[rows, :] = ref[:, qw:mid].astype(f32)
        out_ref[rows, :] = ref[:, mid + parts * 128 :].astype(f32)
        for k in range(size // piece):
            row = first + k * piece
            low = pl.multiple_of(lax.rem(row, kv_rows), piece)
            for d in range(parts):
                col = pl.multiple_of(d * kv_cols + row // kv_rows * 128, 128)
                value = ref[k * piece : (k + 1) * piece, mid + d * 128 : mid + (d + 1) * 128]
                up_ref[pl.ds(low, piece), pl.ds(col, 128)] = value.astype(f32)
    cols = mid_ref[...].T
    down_ref[...] = cols[:kvw, :]
    one_ref[...] = cols[kvw : kvw + 1, :]
    two_ref[...] = cols[kvw + 1 : kvw + 2, :]
    kv_ref[...] = cols[kvw + 2 : kvw + 3, :kv_rows]


def local(
    tokens,
    segments,
    routes,
    gate_scores,
    attn_gain,
    w_query,
    w_down_kv,
    kv_gain,
    w_up_kv,
    w_out,
    ffn_gain,
    w_gate,
    w_up,
    w_down,
    cotangent,
):
    parts = lax.axis_size(SHARD)
    rows, width = tokens.shape
    length = rows * parts
    experts, _, units = w_gate.shape
    d_rows, kvw = w_down_kv.shape
    qw = w_query.shape[1] // parts
    kv_rows, kv_cols = w_up_kv.shape[0], w_up_kv.shape[1] // parts
    zh, y, core = (lax.axis_index(name) for name in REP)
    highs, places, cores = (lax.axis_size(name) for name in REP)
    sub = d_rows // (places * cores)
    at = jnp.stack(
        [lax.axis_index("x"), lax.axis_index("zl"), y, core, (y * cores + core) * sub]
    ).astype(jnp.int32)
    ids = lax.dynamic_slice_in_dim(segments, lax.axis_index(REP) * length, length)
    cosine, sine_tab = rotary_tables(jnp.arange(length, dtype=jnp.int32), DR)
    cosine = jnp.concatenate([cosine, cosine], 1)
    sine_tab = jnp.concatenate([sine_tab, sine_tab], 1)

    chosen = routes[:, :, None] == jnp.arange(EXPERTS, dtype=jnp.int32)[None, None, :]
    routed = jnp.sum(jnp.where(chosen, gate_scores.astype(f32)[:, :, None], 0.0), axis=1)
    cat = qw + kvw + DR
    wide = cat + 128
    tail = [attn_gain, ffn_gain, routed.astype(bf16).reshape(-1), kv_gain]
    row = jnp.concatenate(tail)
    row = jnp.pad(row, (0, wide - row.shape[0]))[None, :]
    chunk = on_core(
        functools.partial(chunk_kernel, sub=sub, qw=qw, kvw=kvw),
        jax.ShapeDtypeStruct((parts, sub + 16, wide), bf16),
        [SM] + [VM] * 4,
        0,
        4 * MIB,
    )(at, w_query, w_down_kv, w_up_kv, row)
    chunk = lax.all_to_all(chunk, SHARD, split_axis=0, concat_axis=0, tiled=True)
    ring = ring_gather(chunk[:, :sub])
    blocks = gather_pairs(tokens, first=chunk)
    pieces, places_of = [], []
    for step, low, block in ring:
        pieces += [block, swap(block)] if cores > 1 else [block]
        places_of += [(step, low, n) for n in range(cores)]
    held, late = lax.optimization_barrier((blocks[2][0], cotangent))
    blocks[2] = (held, blocks[2][1])
    cot = whole_third(whole_second(whole_first(late)))
    cat_w, up_kv_w = on_core(
        functools.partial(weights_kernel, places=places, cores=cores, sub=sub, spots=places_of),
        (
            jax.ShapeDtypeStruct((parts * d_rows, cat), bf16),
            jax.ShapeDtypeStruct((parts * kv_rows, kv_cols), bf16),
        ),
        [SM] + [VM] * len(pieces),
        0,
        10 * MIB,
    )(at, *pieces)
    tail_rows = chunk[:, sub].astype(f32)
    ends = [d_rows, 2 * d_rows, 2 * d_rows + rows * EXPERTS]
    gain_one = tail_rows[:, : ends[0]].reshape(1, -1)
    gain_two = tail_rows[:, ends[0] : ends[1]].reshape(1, -1)
    routed_all = to_relative(tail_rows[:, ends[1] : ends[2]].reshape(parts, rows, EXPERTS))
    gain_kv = tail_rows[:, ends[2] : ends[2] + kv_rows].reshape(1, -1)

    normed = on_core(
        functools.partial(norm_kernel, spots=spots_of(blocks)),
        jax.ShapeDtypeStruct((length, width), bf16),
        [VM] * (1 + len(blocks)),
        0,
        8 * MIB,
    )(gain_one, *[v for v, _ in blocks])
    pre = dot(normed, cat_w, (1, 0))
    shape = jax.ShapeDtypeStruct
    queries, latent, key_value, key_rope, log_total, context = on_core(
        forward_kernel,
        (
            shape((length, qw), bf16),
            shape((length, KVL), bf16),
            shape((length, kv_cols), bf16),
            shape((length, 128), bf16),
            shape((2, length, 128), f32),
            shape((length, 2 * DV), bf16),
        ),
        [SM] + [VM] * 7,
        0,
        10 * MIB,
    )(at, pre, gain_kv, up_kv_w, cosine, sine_tab, ids[:, None], ids[None, :])
    context, cot = lax.optimization_barrier((context, cot))
    grad_out_all = assemble([(v, ((x, 0, z), (x, 1, z))) for (x, z), v in cot.items()])
    inputs_f = tokens.astype(f32)
    residual = inputs_f + merged_rows(dot(context, w_out, (1, 0)).astype(bf16))
    normed_two, inverse_two = norm_parts(residual)
    ffn_own = (normed_two * gain_two).astype(bf16)
    ffn_in = assemble(gather_pairs(ffn_own))

    gate_t = jnp.swapaxes(w_gate, 1, 2).reshape(experts * units, width)
    up_t = jnp.swapaxes(w_up, 1, 2).reshape(experts * units, width)
    down_t = w_down.reshape(experts * units, width)
    expert_of = (jnp.arange(experts * units, dtype=jnp.int32) // units)[None, :]
    weight_cols = jnp.ones((length, experts * units), f32)
    for m in range(EXPERTS):
        weight_cols = jnp.where(expert_of == SHARED + m, routed_all[:, m : m + 1], weight_cols)
    gate_pre = dot(ffn_in, gate_t, (1, 1))
    up_pre = dot(ffn_in, up_t, (1, 1))
    sig = jax.nn.sigmoid(gate_pre)
    hidden = (gate_pre * sig * up_pre * weight_cols).astype(bf16)
    grad_hidden = dot(grad_out_all, down_t, (1, 1))
    scaled = grad_hidden * weight_cols
    grad_gate = (scaled * up_pre * sig * (1.0 + gate_pre * (1.0 - sig))).astype(bf16)
    grad_up = (scaled * gate_pre * sig).astype(bf16)
    grad_ffn = (dot(grad_gate, gate_t, (1, 0)) + dot(grad_up, up_t, (1, 0))).astype(bf16)
    grad_ffn, hidden, grad_gate, grad_up = lax.optimization_barrier(
        (grad_ffn, hidden, grad_gate, grad_up)
    )
    ffn_part = dot(hidden, down_t, (1, 0)).astype(bf16)
    tie = lax.optimization_barrier

    def products(found):
        _, gate, up_ = tie((found[0], grad_gate, grad_up))
        return dot(gate, ffn_in, (0, 0)).astype(bf16), dot(up_, ffn_in, (0, 0)).astype(bf16)

    def packed(found):
        down_part, (gate_part, up_part) = found
        return expert_pack(at, (gate_part, up_part, down_part), places, cores)

    grad_ffn, _, _, (ex_own, *ex_other) = merged_rows(
        grad_ffn,
        (
            lambda found: dot(hidden, grad_out_all, (0, 0)).astype(bf16),
            products,
            packed,
        ),
    )
    ex_got = [swap(v) for v in ex_other]
    gain_two_part = jnp.sum(grad_ffn * normed_two, axis=0)
    grad_residual = cotangent.astype(f32) + norm_back(grad_ffn * gain_two, normed_two, inverse_two)
    blocks, (ex_own, out_parts) = gather_pairs(
        grad_residual.astype(bf16),
        ex_got,
        ffn_part,
        lambda got: (add(ex_own, *got).astype(bf16), scatter_parts(ffn_part)),
    )
    ex_own = [ex_own[r] for r in range(places)]
    ex_got = ring_first(ex_own)
    grad_branch = assemble(blocks)
    grad_branch, out_parts = tie((grad_branch, out_parts))
    out_sent = scatter_sends(out_parts)

    out_part = dot(context, grad_branch, (0, 0)).astype(bf16)
    grad_context = dot(grad_branch, w_out, (1, 1)).astype(bf16)
    grad_pre, grad_key_value = on_core(
        backward_kernel,
        (shape((length, cat), bf16), shape((length, kv_cols), bf16)),
        [SM] + [VM] * 12,
        0,
        15 * MIB,
        [
            pltpu.VMEM((length, 2 * DN), f32),
            pltpu.VMEM((length, 128), f32),
            pltpu.VMEM((length, 256), f32),
            pltpu.VMEM((length, DV), f32),
            pltpu.VMEM((length, 128), f32),
        ],
    )(
        at, grad_context, queries, key_value, key_rope, log_total, pre, gain_kv, up_kv_w,
        cosine, sine_tab, ids[:, None], ids[None, :],
    )
    grad_pre, ex_got, out_sent = tie((grad_pre, ex_got, out_sent))
    ex_own = ring_second(ex_own, ex_got)
    up_kv_part = dot(latent, grad_key_value, (0, 0))
    size = d_rows // (places * cores)
    slabs = width // cat
    last = parts - 1
    sends = pl.pallas_call(
        functools.partial(sends_kernel, places=places, cores=cores, parts=parts),
        out_shape=[shape((places, parts + slabs, size, wide), bf16)] * cores,
        grid=(parts + slabs,),
        in_specs=[
            SM,
            pl.BlockSpec((length, d_rows), lambda d: (0, jnp.minimum(d, last))),
            pl.BlockSpec((length, cat), lambda d: (0, 0)),
            pl.BlockSpec((d_rows, cat), lambda d: (jnp.minimum(d, last), 0)),
            pl.BlockSpec((kv_rows, kv_cols), lambda d: (jnp.minimum(d, last), 0)),
            pl.BlockSpec((kv_rows, kv_cols), lambda d: (jnp.minimum(d, last), 0)),
            pl.BlockSpec((d_rows, 1), lambda d: (jnp.minimum(d, last), 0)),
            pl.BlockSpec((kv_rows, 1), lambda d: (jnp.minimum(d, last), 0)),
            pl.BlockSpec((d_rows, 1), lambda d: (jnp.minimum(d, last), 0)),
            pl.BlockSpec((d_rows, cat), lambda d: (0, jnp.maximum(d - parts, 0))),
        ],
        out_specs=[pl.BlockSpec((places, 1, size, wide), lambda d: (0, d, 0, 0))] * cores,
        scratch_shapes=[pltpu.VMEM((d_rows, wide), bf16)],
        compiler_params=pltpu.CompilerParams(vmem_limit_bytes=40 * MIB),
        cost_estimate=pl.CostEstimate(flops=0, bytes_accessed=16 * MIB, transcendentals=0),
    )(
        at, normed, grad_pre, cat_w, up_kv_part, up_kv_w,
        gain_one.reshape(-1, 1), gain_kv.reshape(-1, 1), gain_two_part.reshape(-1, 1), out_part,
    )
    sends, out_sent, ex_own = tie((sends, out_sent, ex_own))
    own, *other = sends
    got = [swap(v) for v in other]
    ex_own = add(*ex_own).astype(bf16)
    ex_got = ex_own
    if highs > 1:
        ex_own = ex_own.reshape(highs, -1, ex_own.shape[1])
        ex_got = hop(pick(ex_own, 1 - zh, 0))
        ex_own = pick(ex_own, zh, 0)
    out_sent = scatter_second(out_parts, out_sent)
    normed_part = dot(grad_pre, cat_w, (1, 1)).astype(bf16)
    x_parts, x_sent = scatter_first(normed_part)
    got, ex_got = tie((got, ex_got))
    own = add(own, *got).astype(bf16)
    own = [own[r] for r in range(places)]
    got = ring_first(own)
    if highs > 1:
        ex_own = add(ex_own, ex_got).astype(bf16)
        ex_got = hop(ex_own)
    got, out_sent = tie((got, out_sent))
    own = ring_second(own, got)
    out_sent = scatter_third(*out_sent)
    own, ex_got = tie((own, ex_got))
    if highs > 1:
        low = jnp.where(zh == 0, ex_own, ex_got)
        ex_own = jnp.concatenate([low, jnp.where(zh == 0, ex_got, ex_own)], 0)
    pairs = {0: [swap(ex_own)] if cores > 1 else []}
    own = add(*own).astype(bf16)
    got = own
    if highs > 1:
        own = own.reshape(parts + slabs, highs, size // highs, wide)
        got = hop(pick(own, 1 - zh, 1))
        own = pick(own, zh, 1)
    ring = {0: ex_own}
    if places > 1:
        ring[3], ring[1] = up(ex_own), down(ex_own)
    got, x_sent, out_sent = tie((got, x_sent, out_sent))
    if highs > 1:
        own = add(own, got).astype(bf16)
    x_sent = scatter_second(x_parts, x_sent)
    out_own = own[parts:]
    own = lax.all_to_all(own[:parts], SHARD, split_axis=0, concat_axis=0, tiled=True)
    own, out_own, ring, pairs, x_sent = tie((own, out_own, ring, pairs, x_sent))
    own = on_core(
        functools.partial(join_kernel, qw=qw, cat=cat),
        shape((own.shape[1], parts * (qw + 128) + cat - qw + slabs * cat), bf16),
        [VM, VM],
        0,
        MIB,
    )(own, out_own)
    own, ring = tie((own, ring))
    pair = own
    if highs > 1:
        got = hop(own)
    output = (residual + add(*out_sent)).astype(bf16)
    if places > 1:
        half = ring[0].shape[0] // 2
        ring[2] = (up(ring[3][:half]), down(ring[1][half:]))
    for r in (1, 3) if places > 1 else ():
        pairs[r] = [swap(ring[r])] if cores > 1 else []
    if highs > 1:
        got, ring, pairs = tie((got, ring, pairs))
        pair = jnp.where(zh == 0, jnp.concatenate([own, got], 0), jnp.concatenate([got, own], 0))
    x_sent = scatter_third(*x_sent)
    grads = expert_unpack(at, 0, [ex_own, *pairs[0]], (), places, experts * units, width)
    whole = {0: pair}

    def input_grad(sent):
        own_one, inverse_one = norm_parts(inputs_f)
        return grad_residual + norm_back(add(*sent) * gain_one, own_one, inverse_one)

    if places == 1:
        tokens_grad = input_grad(x_sent)
    if places > 1:
        whole[3], whole[1] = up(pair), down(pair)
        ring[2] = jnp.concatenate(ring[2], 0)
        pairs[2] = [swap(ring[2])] if cores > 1 else []
        for r in (1, 3):
            grads = expert_unpack(at, r, [ring[r], *pairs[r]], grads, places, experts * units, width)
        whole, grads, pairs, x_sent = tie((whole, grads, pairs, x_sent))
        half = pair.shape[0] // 2
        across = (up(whole[3][:half]), down(whole[1][half:]))
        tokens_grad = input_grad(x_sent)
        grads = expert_unpack(at, 2, [ring[2], *pairs[2]], grads, places, experts * units, width)
        across, grads, tokens_grad = tie((across, grads, tokens_grad))
        whole[2] = jnp.concatenate(across, 0)
    pieces = []
    for r in range(places):
        pieces += [whole[r], swap(whole[r])] if cores > 1 else [whole[r]]
    gate_sum, up_sum, down_sum = [v.reshape(experts, units, width) for v in grads]
    query_sum, down_kv_sum, one_sum, two_sum, kv_sum, up_kv_sum, out_sum = on_core(
        functools.partial(unpack_kernel, places=places, cores=cores, size=size, parts=parts),
        (
            shape((d_rows, parts * qw), f32),
            shape((kvw, d_rows), f32),
            shape((1, d_rows), f32),
            shape((1, d_rows), f32),
            shape((1, kv_rows), f32),
            shape((kv_rows, parts * kv_cols), f32),
            shape((d_rows, width), f32),
        ),
        [SM] + [VM] * (places * cores),
        0,
        12 * MIB,
        [pltpu.VMEM((d_rows, kvw + DR), f32)],
    )(at, *pieces)
    return (
        output,
        tokens_grad,
        one_sum.reshape(-1),
        query_sum,
        down_kv_sum.T,
        kv_sum.reshape(-1),
        up_kv_sum,
        out_sum,
        two_sum.reshape(-1),
        jnp.swapaxes(gate_sum, 1, 2),
        jnp.swapaxes(up_sum, 1, 2),
        down_sum,
    )


def split_mesh(mesh):
    reps = mesh.shape["rep"]
    shards = mesh.shape["shard"]
    zh, core = (2, 2) if reps % 4 == 0 else (1, 1)
    zl = 2 if shards % 2 == 0 else 1
    shape = (zh, reps // (zh * core), core, shards // zl, zl)
    return Mesh(mesh.devices.reshape(shape), REP + SHARD)


def solution(mesh):
    every = REP + SHARD
    in_specs = (
        P(every, None),
        P(),
        P(every, None),
        P(every, None),
        P(SHARD),
        P(SHARD, None),
        P(SHARD, None),
        P(SHARD),
        P(SHARD, None),
        P(SHARD, None),
        P(SHARD),
        P(None, None, SHARD),
        P(None, None, SHARD),
        P(None, SHARD, None),
        P(every, None),
    )
    out_specs = (
        P(every, None),
        P(every, None),
        P(SHARD),
        P(SHARD, None),
        P(SHARD, None),
        P(SHARD),
        P(SHARD, None),
        P(SHARD, None),
        P(SHARD),
        P(None, None, SHARD),
        P(None, None, SHARD),
        P(None, SHARD, None),
    )
    return jax.shard_map(
        local, mesh=split_mesh(mesh), in_specs=in_specs, out_specs=out_specs, check_vma=False
    )
```
